32 devices in a mesh: groups: 2 (over x), mp: 16 (over z, y, core).
Axes of the slice: x: 2, y: 2, z: 4, core: 2. Of those that a mesh axis runs over, the one named last changes fastest.
Arguments:
- up_pre: bfloat16 [96, 36864], P(('groups', 'mp')), parts along dimension 0, may hold values from -6 to 6
- down_weight: bfloat16 [36864, 18432], P('mp'), may hold values from -0.03125 to 0.03125
Outputs:
- mixed: bfloat16 [96, 18432], P(('groups', 'mp')), parts along dimension 0
The draws below stay inside these ranges and needn't reach their ends.
There are 2 independent parts, one for each index of `groups`. The reference program is written for one: setup_inputs(seed, part) draws one part's arguments, and reference() takes and returns one part's arrays. A program takes and returns all parts, laid end to end along the dimension named above; an argument that names none is the same for every part. Nothing has to cross between parts.
All inputs are finite; a program needn't handle non-finite values.
Results may differ from the reference program's by a relative error of at most 0.0049.
Values may be sent and summed in bfloat16 or wider, within the bound.
A program may use at most 192 MiB of HBM per device.

```python
import jax
import jax.numpy as jnp

D = 18432
FF = 36864
TOKENS = 48


def shard_levels(key, extent, shards, least, largest):
    factor_of = 1.0
    for dim, blocks in shards:
        draws = jax.random.uniform(jax.random.fold_in(jax.random.fold_in(key, 6), dim), (blocks,), jnp.float32, least / len(shards), largest / len(shards))
        factor_of = factor_of * jnp.repeat(jnp.exp(draws), extent[dim] // blocks).reshape((-1,) + (1,) * (len(extent) - 1 - dim))
    return factor_of


def bell_draw(key, dims, deviation, most, cuts=(), held_as=jnp.bfloat16):
    entries = deviation * jax.random.normal(key, dims, jnp.float32)
    if cuts:
        entries = entries * shard_levels(key, dims, cuts, -0.22, 0.18)
    return jnp.clip(entries, -most, most).astype(held_as)


def setup_inputs(seed: int = 0, part: int = 0) -> dict:
    streams_of = jax.random.split(jax.random.key(seed), 3)
    part_splits = jax.random.split(jax.random.fold_in(streams_of[2], part), 3)
    return {
        "up_pre": bell_draw(part_splits[0], (TOKENS, FF), 1.0, 6.0, ((0, 16),)),
        "down_weight": bell_draw(streams_of[1], (FF, D), FF ** -0.5, 0.03125, ((0, 16),)),
    }


def reference(up_pre, down_weight):
    up = up_pre.astype(jnp.float32)
    positive = jnp.maximum(up, 0.0)
    hidden = (positive * positive).astype(jnp.bfloat16)
    return jnp.dot(hidden, down_weight, preferred_element_type=jnp.float32).astype(jnp.bfloat16)
```

```python
import functools

import jax
import jax.numpy as jnp
from jax import lax
from jax.experimental import pallas as pl
from jax.experimental.pallas import tpu as pltpu
from jax.sharding import PartitionSpec as P

MESH = pl.DeviceIdType.MESH


def squared_relu(up_vals):
    positive = jnp.maximum(up_vals.astype(jnp.float32), 0.0)
    return (positive * positive).astype(jnp.bfloat16)


def plain_body(up_pre, down_weight):
    up_cols = lax.all_to_all(up_pre, "mp", split_axis=1, concat_axis=0, tiled=True)
    hidden = squared_relu(up_cols)
    summed = lax.psum_scatter(
        jnp.dot(hidden, down_weight, preferred_element_type=jnp.float32),
        "mp",
        scatter_dimension=0,
        tiled=True,
    )
    return summed.astype(jnp.bfloat16)


def kernel(n, up_ref, w_ref, out_ref, wbuf, upbuf, hid32, hid, yb, asend, arecv, bsend, brecv, csend, crecv, own, fin,
           w_sem, up_ssem, up_rsem, own_sem, a_ssem, a_rsem, b_ssem, b_rsem, c_ssem, c_rsem, f_ssem, f_rsem, fl_sem):
    nz = n // 4
    chunks = n // 2
    x = lax.axis_index("groups")
    p = lax.axis_index("mp")
    me = x * n + p
    chip, core = p // 2, p % 2
    z, y = chip // 2, chip % 2
    rows, depth, width = up_ref.shape[0], w_ref.shape[0], wbuf.shape[2]
    group_rows = rows * n
    half = width * chunks

    def cols_of(x_part, chunk):
        return pl.ds(pl.multiple_of(x_part * half + chunk * width, 128), width)

    def chunk_of(t):
        zt = lax.rem(z + 1 + t // 2, nz)
        yt = jnp.where(t % 2 == 0, 1 - y, y)
        return zt * 2 + yt

    def w_copy(t):
        return pltpu.make_async_copy(w_ref.at[:, cols_of(x, chunk_of(t))], wbuf.at[t], w_sem.at[t])

    def start_w(t, _):
        w_copy(t).start()
        return 0

    lax.fori_loop(0, chunks, start_w, 0)

    barrier = pltpu.get_barrier_semaphore()

    def greet(d, _):
        other = lax.rem(me + d, 2 * n)
        pl.semaphore_signal(barrier, inc=1, device_id=(other // n, lax.rem(other, n)), device_id_type=MESH)
        return 0

    lax.fori_loop(1, 2 * n, greet, 0)

    def up_cols(q):
        return up_ref.at[:, pl.ds(pl.multiple_of(q * depth, 128), depth)]

    def up_copy(d, slot):
        other = lax.rem(me + d, 2 * n)
        q = lax.rem(other, n)
        return pltpu.make_async_remote_copy(
            src_ref=up_cols(q), dst_ref=upbuf.at[slot], send_sem=up_ssem.at[d], recv_sem=up_rsem.at[slot],
            device_id=(other // n, q), device_id_type=MESH)

    own_up = pltpu.make_async_copy(up_cols(p), upbuf.at[me], own_sem)
    own_up.start()
    pl.semaphore_wait(barrier, 2 * n - 1)

    def start_up(d, _):
        up_copy(d, me).start()
        return 0

    lax.fori_loop(1, 2 * n, start_up, 0)
    own_up.wait()

    def wait_up(d, _):
        up_copy(d, lax.rem(me + 2 * n - d, 2 * n)).wait_recv()
        return 0

    lax.fori_loop(1, 2 * n, wait_up, 0)
    for s in range(2 * n):
        positive = jnp.maximum(upbuf[s].astype(jnp.float32), 0.0)
        hid32[s * rows:(s + 1) * rows, :] = positive * positive
    hid[...] = hid32[...].astype(jnp.bfloat16)

    def a_copy(t):
        return pltpu.make_async_remote_copy(
            src_ref=asend.at[t], dst_ref=arecv.at[t], send_sem=a_ssem.at[t], recv_sem=a_rsem.at[t],
            device_id=(x, chip * 2 + 1 - core), device_id_type=MESH)

    def b_copy(j):
        return pltpu.make_async_remote_copy(
            src_ref=bsend.at[j], dst_ref=brecv.at[j], send_sem=b_ssem.at[j], recv_sem=b_rsem.at[j],
            device_id=(x, (z * 2 + 1 - y) * 2 + core), device_id_type=MESH)

    def c_copy(j):
        return pltpu.make_async_remote_copy(
            src_ref=csend.at[j], dst_ref=crecv.at[j], send_sem=c_ssem.at[j], recv_sem=c_rsem.at[j],
            device_id=(x, (lax.rem(z + 1 + j, nz) * 2 + y) * 2 + core), device_id_type=MESH)

    def step(t, _):
        @pl.when(t < chunks)
        def _():
            w_copy(t).wait()
            prod = jnp.dot(hid[...], wbuf[t], preferred_element_type=jnp.float32)
            yb[t % 2, 0] = prod[:group_rows]
            yb[t % 2, 1] = prod[group_rows:]
            asend[t] = yb[t % 2, 1 - core].astype(jnp.bfloat16)
            a_copy(t).start()

        @pl.when(t >= 1)
        def _():
            u = t - 1
            j = u // 2
            a_copy(u).wait_recv()
            total = yb[u % 2, core] + arecv[u].astype(jnp.float32)

            @pl.when(u % 2 == 0)
            def _():
                bsend[j] = total.astype(jnp.bfloat16)
                b_copy(j).start()

            @pl.when(u % 2 == 1)
            def _():
                b_copy(j).wait_recv()
                both = total + brecv[j].astype(jnp.float32)

                @pl.when(j < nz - 1)
                def _():
                    csend[j] = both.astype(jnp.bfloat16)
                    c_copy(j).start()

                @pl.when(j == nz - 1)
                def _():
                    own[...] = both

        return 0

    lax.fori_loop(0, chunks + 1, step, 0)

    for j in range(nz - 1):
        c_copy(j).wait_recv()
    total = own[...]
    for j in range(nz - 1):
        total = total + crecv[j].astype(jnp.float32)
    for q in range(n):
        fin[q] = total[q * rows:(q + 1) * rows].astype(jnp.bfloat16)

    def f_copy(q, x_part, chunk):
        return pltpu.make_async_remote_copy(
            src_ref=fin.at[q], dst_ref=out_ref.at[:, cols_of(x_part, chunk)], send_sem=f_ssem.at[q],
            recv_sem=f_rsem.at[x_part * chunks + chunk], device_id=(core, q), device_id_type=MESH)

    mine = pltpu.make_async_copy(fin.at[p], out_ref.at[:, cols_of(x, chip)], fl_sem)

    @pl.when(x == core)
    def _():
        mine.start()

    def each_final(q, act):
        @pl.when(jnp.logical_or(x != core, q != p))
        def _():
            act(f_copy(q, x, chip))

    def start_final(i, _):
        each_final(lax.rem(p + i, n), lambda c: c.start())
        return 0

    lax.fori_loop(0, n, start_final, 0)

    def wait_final(i, _):
        x_part, chunk = i // chunks, lax.rem(i, chunks)

        @pl.when(jnp.logical_or(x_part != x, chunk * 2 + x != p))
        def _():
            f_copy(i, x_part, chunk).wait_recv()

        return 0

    lax.fori_loop(0, n, wait_final, 0)

    @pl.when(x == core)
    def _():
        mine.wait()

    def end_up(d, _):
        up_copy(d, me).wait_send()
        return 0

    def end_a(t, _):
        a_copy(t).wait_send()
        return 0

    def end_final(q, _):
        each_final(q, lambda c: c.wait_send())
        return 0

    lax.fori_loop(1, 2 * n, end_up, 0)
    lax.fori_loop(0, chunks, end_a, 0)
    for j in range(nz):
        b_copy(j).wait_send()
    for j in range(nz - 1):
        c_copy(j).wait_send()
    lax.fori_loop(0, n, end_final, 0)


def fused_body(n, up_pre, down_weight):
    rows = up_pre.shape[0]
    depth, model = down_weight.shape
    nz, chunks, tokens = n // 4, n // 2, rows * n
    width = model // n
    bf, f32, dma = jnp.bfloat16, jnp.float32, pltpu.SemaphoreType.DMA
    return pl.pallas_call(
        functools.partial(kernel, n),
        out_shape=jax.ShapeDtypeStruct((rows, model), bf),
        in_specs=[pl.BlockSpec(memory_space=pl.ANY)] * 2,
        out_specs=pl.BlockSpec(memory_space=pl.ANY),
        scratch_shapes=[
            pltpu.VMEM((chunks, depth, width), bf),
            pltpu.VMEM((2 * n, rows, depth), bf),
            pltpu.VMEM((2 * tokens, depth), f32),
            pltpu.VMEM((2 * tokens, depth), bf),
            pltpu.VMEM((2, 2, tokens, width), f32),
            pltpu.VMEM((chunks, tokens, width), bf),
            pltpu.VMEM((chunks, tokens, width), bf),
            pltpu.VMEM((nz, tokens, width), bf),
            pltpu.VMEM((nz, tokens, width), bf),
            pltpu.VMEM((nz - 1, tokens, width), bf),
            pltpu.VMEM((nz - 1, tokens, width), bf),
            pltpu.VMEM((tokens, width), f32),
            pltpu.VMEM((n, rows, width), bf),
            dma((chunks,)), dma((2 * n,)), dma((2 * n,)), dma,
            dma((chunks,)), dma((chunks,)), dma((nz,)), dma((nz,)), dma((nz - 1,)), dma((nz - 1,)),
            dma((n,)), dma((n,)), dma,
        ],
        compiler_params=pltpu.CompilerParams(collective_id=0, has_side_effects=True, vmem_limit_bytes=60 * 2 ** 20),
        cost_estimate=pl.CostEstimate(flops=4 * tokens * depth * model // 2, bytes_accessed=depth * model, transcendentals=0),
    )(up_pre, down_weight)


def solution(mesh):
    in_specs = (P(("groups", "mp"), None), P("mp", None))
    out_specs = P(("groups", "mp"), None)
    n = mesh.shape["mp"]

    def body(up_pre, down_weight):
        depth, model = down_weight.shape
        resident = depth * model
        fits = mesh.shape["groups"] == 2 and n == 16 and (up_pre.shape[0] * n) % 16 == 0
        if fits and model % (128 * n) == 0 and depth % 128 == 0 and resident <= 44 * 2 ** 20:
            return fused_body(n, up_pre, down_weight)
        return plain_body(up_pre, down_weight)

    return jax.shard_map(body, mesh=mesh, in_specs=in_specs, out_specs=out_specs, check_vma=False)
```

```python
import functools

import jax
import jax.numpy as jnp
from jax import lax
from jax.experimental import pallas as pl
from jax.experimental.pallas import tpu as pltpu
from jax.sharding import PartitionSpec as P

MESH = pl.DeviceIdType.MESH
LAG_A, LAG_B = 1, 2


def squared_relu(up_vals):
    positive = jnp.maximum(up_vals.astype(jnp.float32), 0.0)
    return (positive * positive).astype(jnp.bfloat16)


def plain_body(up_pre, down_weight):
    up_cols = lax.all_to_all(up_pre, "mp", split_axis=1, concat_axis=0, tiled=True)
    hidden = squared_relu(up_cols)
    summed = lax.psum_scatter(
        jnp.dot(hidden, down_weight, preferred_element_type=jnp.float32),
        "mp",
        scatter_dimension=0,
        tiled=True,
    )
    return summed.astype(jnp.bfloat16)


def kernel(n, up_ref, w_ref, out_ref, wbuf, upbuf, hid32, hid, ykeep, asend, arecv, bkeep, bsend, brecv, csend, crecv, own, fin,
           w_sem, up_ssem, up_rsem, fw_ssem, fw_rsem, own_sem, a_ssem, a_rsem, b_ssem, b_rsem, c_ssem, c_rsem, f_ssem, f_rsem, fl_sem):
    nz = n // 4
    chunks = n // 2
    x = lax.axis_index("groups")
    p = lax.axis_index("mp")
    me = x * n + p
    chip, core = p // 2, p % 2
    z, y = chip // 2, chip % 2
    rows, depth, width = up_ref.shape[0], w_ref.shape[0], wbuf.shape[2]
    group_rows = rows * n
    half = width * chunks

    def cols_of(x_part, chunk):
        return pl.ds(pl.multiple_of(x_part * half + chunk * width, 128), width)

    def chunk_of(t):
        zt = lax.rem(z + 1 + t // 2, nz)
        yt = jnp.where(t % 2 == 0, 1 - y, y)
        return zt * 2 + yt

    def w_copy(t):
        return pltpu.make_async_copy(w_ref.at[:, cols_of(x, chunk_of(t))], wbuf.at[t], w_sem.at[t])

    def start_w(t, _):
        w_copy(t).start()
        return 0

    lax.fori_loop(0, chunks, start_w, 0)

    barrier = pltpu.get_barrier_semaphore()

    def greet(d, _):
        other = lax.rem(me + d, 2 * n)
        pl.semaphore_signal(barrier, inc=1, device_id=(other // n, lax.rem(other, n)), device_id_type=MESH)
        return 0

    lax.fori_loop(1, 2 * n, greet, 0)

    def up_cols(q):
        return up_ref.at[:, pl.ds(pl.multiple_of(q * depth, 128), depth)]

    def up_copy(d, slot):
        q = lax.rem(p + d, n)
        return pltpu.make_async_remote_copy(
            src_ref=up_cols(q), dst_ref=upbuf.at[0, slot], send_sem=up_ssem.at[d], recv_sem=up_rsem.at[slot],
            device_id=(x, q), device_id_type=MESH)

    def forward(s):
        return pltpu.make_async_remote_copy(
            src_ref=upbuf.at[0, s], dst_ref=upbuf.at[1, s], send_sem=fw_ssem.at[s], recv_sem=fw_rsem.at[s],
            device_id=(1 - x, p), device_id_type=MESH)

    own_up = pltpu.make_async_copy(up_cols(p), upbuf.at[0, p], own_sem)
    own_up.start()
    pl.semaphore_wait(barrier, 2 * n - 1)

    def start_up(d, _):
        up_copy(d, p).start()
        return 0

    lax.fori_loop(1, n, start_up, 0)
    own_up.wait()
    forward(p).start()

    def pass_on(d, _):
        s = lax.rem(p + n - d, n)
        up_copy(d, s).wait_recv()
        forward(s).start()
        return 0

    lax.fori_loop(1, n, pass_on, 0)
    for part in range(2):
        if part == 1:
            for s in range(n):
                forward(s).wait_recv()
        for s in range(n):
            row = part * group_rows + s * rows
            positive = jnp.maximum(upbuf[part, s].astype(jnp.float32), 0.0)
            hid32[row:row + rows, :] = positive * positive
        span = slice(part * group_rows, (part + 1) * group_rows)
        hid[span, :] = hid32[span, :].astype(jnp.bfloat16)
    keep = lax.rem(x + core, 2)

    def a_copy(t):
        return pltpu.make_async_remote_copy(
            src_ref=asend.at[t], dst_ref=arecv.at[t], send_sem=a_ssem.at[t], recv_sem=a_rsem.at[t],
            device_id=(x, chip * 2 + 1 - core), device_id_type=MESH)

    def b_copy(j):
        return pltpu.make_async_remote_copy(
            src_ref=bsend.at[j], dst_ref=brecv.at[j], send_sem=b_ssem.at[j], recv_sem=b_rsem.at[j],
            device_id=(x, (z * 2 + 1 - y) * 2 + core), device_id_type=MESH)

    def c_copy(j):
        return pltpu.make_async_remote_copy(
            src_ref=csend.at[j], dst_ref=crecv.at[j], send_sem=c_ssem.at[j], recv_sem=c_rsem.at[j],
            device_id=(x, (lax.rem(z + 1 + j, nz) * 2 + y) * 2 + core), device_id_type=MESH)

    def step(t, _):
        @pl.when(t < chunks)
        def _():
            w_copy(t).wait()
            prod = jnp.dot(hid[...], wbuf[t], preferred_element_type=jnp.float32)
            ykeep[t, 0] = prod[:group_rows]
            ykeep[t, 1] = prod[group_rows:]
            asend[t] = ykeep[t, 1 - keep].astype(jnp.bfloat16)
            a_copy(t).start()

        u = t - LAG_A

        @pl.when(jnp.logical_and(u >= 0, u < chunks))
        def _():
            a_copy(u).wait_recv()
            total = ykeep[u, keep] + arecv[u].astype(jnp.float32)
            j = u // 2

            @pl.when(u % 2 == 0)
            def _():
                bsend[j] = total.astype(jnp.bfloat16)
                b_copy(j).start()

            @pl.when(u % 2 == 1)
            def _():
                bkeep[j] = total

        v = t - LAG_A - LAG_B

        @pl.when(jnp.logical_and(v >= 0, v % 2 == 1))
        def _():
            j = v // 2
            b_copy(j).wait_recv()
            both = bkeep[j] + brecv[j].astype(jnp.float32)

            @pl.when(j < nz - 1)
            def _():
                csend[j] = both.astype(jnp.bfloat16)
                c_copy(j).start()

            @pl.when(j == nz - 1)
            def _():
                own[...] = both

        return 0

    lax.fori_loop(0, chunks + LAG_A + LAG_B, step, 0)

    for j in range(nz - 1):
        c_copy(j).wait_recv()
    total = own[...]
    for j in range(nz - 1):
        total = total + crecv[j].astype(jnp.float32)
    for q in range(n):
        fin[q] = total[q * rows:(q + 1) * rows].astype(jnp.bfloat16)

    def f_copy(q, x_part, chunk):
        return pltpu.make_async_remote_copy(
            src_ref=fin.at[q], dst_ref=out_ref.at[:, cols_of(x_part, chunk)], send_sem=f_ssem.at[q],
            recv_sem=f_rsem.at[x_part * chunks + chunk], device_id=(core, q), device_id_type=MESH)

    mine = pltpu.make_async_copy(fin.at[p], out_ref.at[:, cols_of(x, chip)], fl_sem)

    @pl.when(x == core)
    def _():
        mine.start()

    def each_final(q, act):
        @pl.when(jnp.logical_or(x != core, q != p))
        def _():
            act(f_copy(q, x, chip))

    def start_final(i, _):
        each_final(lax.rem(p + i, n), lambda c: c.start())
        return 0

    lax.fori_loop(0, n, start_final, 0)

    def wait_final(i, _):
        x_part, chunk = i // chunks, lax.rem(i, chunks)

        @pl.when(jnp.logical_or(x_part != x, chunk * 2 + x != p))
        def _():
            f_copy(i, x_part, chunk).wait_recv()

        return 0

    lax.fori_loop(0, n, wait_final, 0)

    @pl.when(x == core)
    def _():
        mine.wait()

    def end_up(d, _):
        up_copy(d, p).wait_send()
        return 0

    def end_a(t, _):
        a_copy(t).wait_send()
        return 0

    def end_final(q, _):
        each_final(q, lambda c: c.wait_send())
        return 0

    lax.fori_loop(1, n, end_up, 0)
    for s in range(n):
        forward(s).wait_send()
    lax.fori_loop(0, chunks, end_a, 0)
    for j in range(nz):
        b_copy(j).wait_send()
    for j in range(nz - 1):
        c_copy(j).wait_send()
    lax.fori_loop(0, n, end_final, 0)


def fused_body(n, up_pre, down_weight):
    rows = up_pre.shape[0]
    depth, model = down_weight.shape
    nz, chunks, tokens = n // 4, n // 2, rows * n
    width = model // n
    bf, f32, dma = jnp.bfloat16, jnp.float32, pltpu.SemaphoreType.DMA
    return pl.pallas_call(
        functools.partial(kernel, n),
        out_shape=jax.ShapeDtypeStruct((rows, model), bf),
        in_specs=[pl.BlockSpec(memory_space=pl.ANY)] * 2,
        out_specs=pl.BlockSpec(memory_space=pl.ANY),
        scratch_shapes=[
            pltpu.VMEM((chunks, depth, width), bf),
            pltpu.VMEM((2, n, rows, depth), bf),
            pltpu.VMEM((2 * tokens, depth), f32),
            pltpu.VMEM((2 * tokens, depth), bf),
            pltpu.VMEM((chunks, 2, tokens, width), f32),
            pltpu.VMEM((chunks, tokens, width), bf),
            pltpu.VMEM((chunks, tokens, width), bf),
            pltpu.VMEM((nz, tokens, width), f32),
            pltpu.VMEM((nz, tokens, width), bf),
            pltpu.VMEM((nz, tokens, width), bf),
            pltpu.VMEM((nz - 1, tokens, width), bf),
            pltpu.VMEM((nz - 1, tokens, width), bf),
            pltpu.VMEM((tokens, width), f32),
            pltpu.VMEM((n, rows, width), bf),
            dma((chunks,)), dma((n,)), dma((n,)), dma((n,)), dma((n,)), dma,
            dma((chunks,)), dma((chunks,)), dma((nz,)), dma((nz,)), dma((nz - 1,)), dma((nz - 1,)),
            dma((n,)), dma((n,)), dma,
        ],
        compiler_params=pltpu.CompilerParams(collective_id=0, has_side_effects=True, vmem_limit_bytes=60 * 2 ** 20),
        cost_estimate=pl.CostEstimate(flops=4 * tokens * depth * model // 2, bytes_accessed=depth * model, transcendentals=0),
    )(up_pre, down_weight)


def solution(mesh):
    in_specs = (P(("groups", "mp"), None), P("mp", None))
    out_specs = P(("groups", "mp"), None)
    n = mesh.shape["mp"]

    def body(up_pre, down_weight):
        depth, model = down_weight.shape
        resident = depth * model
        fits = mesh.shape["groups"] == 2 and n == 16 and (up_pre.shape[0] * n) % 16 == 0
        if fits and model % (128 * n) == 0 and depth % 128 == 0 and resident <= 44 * 2 ** 20:
            return fused_body(n, up_pre, down_weight)
        return plain_body(up_pre, down_weight)

    return jax.shard_map(body, mesh=mesh, in_specs=in_specs, out_specs=out_specs, check_vma=False)
```

```python
import functools

import jax
import jax.numpy as jnp
from jax import lax
from jax.experimental import pallas as pl
from jax.experimental.pallas import tpu as pltpu
from jax.sharding import PartitionSpec as P

MESH = pl.DeviceIdType.MESH
LAG_A, LAG_B = 1, 2
EARLY = 4


def squared_relu(up_vals):
    positive = jnp.maximum(up_vals.astype(jnp.float32), 0.0)
    return (positive * positive).astype(jnp.bfloat16)


def plain_body(up_pre, down_weight):
    up_cols = lax.all_to_all(up_pre, "mp", split_axis=1, concat_axis=0, tiled=True)
    hidden = squared_relu(up_cols)
    summed = lax.psum_scatter(
        jnp.dot(hidden, down_weight, preferred_element_type=jnp.float32),
        "mp",
        scatter_dimension=0,
        tiled=True,
    )
    return summed.astype(jnp.bfloat16)


def kernel(n, up_ref, w_ref, out_ref, wbuf, upbuf, hid32, hid, ykeep, asend, arecv, bkeep, bsend, brecv, csend, crecv, own, fin,
           w_sem, up_ssem, up_rsem, fw_ssem, fw_rsem, own_sem, a_ssem, a_rsem, b_ssem, b_rsem, c_ssem, c_rsem, f_ssem, f_rsem, fl_sem):
    nz = n // 4
    chunks = n // 2
    x = lax.axis_index("groups")
    p = lax.axis_index("mp")
    me = x * n + p
    chip, core = p // 2, p % 2
    z, y = chip // 2, chip % 2
    rows, depth, width = up_ref.shape[0], w_ref.shape[0], wbuf.shape[2]
    group_rows = rows * n
    half = width * chunks

    def cols_of(x_part, chunk):
        return pl.ds(pl.multiple_of(x_part * half + chunk * width, 128), width)

    def chunk_of(t):
        zt = lax.rem(z + 1 + t // 2, nz)
        yt = jnp.where(t % 2 == 0, 1 - y, y)
        return zt * 2 + yt

    def w_copy(t):
        return pltpu.make_async_copy(w_ref.at[:, cols_of(x, chunk_of(t))], wbuf.at[t], w_sem.at[t])

    def start_w(t, _):
        w_copy(t).start()
        return 0

    lax.fori_loop(0, EARLY, start_w, 0)

    barrier = pltpu.get_barrier_semaphore()

    def greet(d, _):
        other = lax.rem(me + d, 2 * n)
        pl.semaphore_signal(barrier, inc=1, device_id=(other // n, lax.rem(other, n)), device_id_type=MESH)
        return 0

    lax.fori_loop(1, 2 * n, greet, 0)

    def up_cols(q):
        return up_ref.at[:, pl.ds(pl.multiple_of(q * depth, 128), depth)]

    def up_copy(d, slot):
        q = lax.rem(p + d, n)
        return pltpu.make_async_remote_copy(
            src_ref=up_cols(q), dst_ref=upbuf.at[0, slot], send_sem=up_ssem.at[d], recv_sem=up_rsem.at[slot],
            device_id=(x, q), device_id_type=MESH)

    def forward(s):
        return pltpu.make_async_remote_copy(
            src_ref=upbuf.at[0, s], dst_ref=upbuf.at[1, s], send_sem=fw_ssem.at[s], recv_sem=fw_rsem.at[s],
            device_id=(1 - x, p), device_id_type=MESH)

    own_up = pltpu.make_async_copy(up_cols(p), upbuf.at[0, p], own_sem)
    own_up.start()
    pl.semaphore_wait(barrier, 2 * n - 1)

    def start_up(d, _):
        up_copy(d, p).start()
        return 0

    lax.fori_loop(1, n, start_up, 0)
    own_up.wait()
    forward(p).start()

    def pass_on(d, _):
        s = lax.rem(p + n - d, n)
        up_copy(d, s).wait_recv()
        forward(s).start()
        return 0

    lax.fori_loop(1, n, pass_on, 0)
    lax.fori_loop(EARLY, chunks, start_w, 0)
    for part in range(2):
        if part == 1:
            for s in range(n):
                forward(s).wait_recv()
        for s in range(n):
            row = part * group_rows + s * rows
            positive = jnp.maximum(upbuf[part, s].astype(jnp.float32), 0.0)
            hid32[row:row + rows, :] = positive * positive
        span = slice(part * group_rows, (part + 1) * group_rows)
        hid[span, :] = hid32[span, :].astype(jnp.bfloat16)
    keep = lax.rem(x + core, 2)

    def a_copy(t):
        return pltpu.make_async_remote_copy(
            src_ref=asend.at[t], dst_ref=arecv.at[t], send_sem=a_ssem.at[t], recv_sem=a_rsem.at[t],
            device_id=(x, chip * 2 + 1 - core), device_id_type=MESH)

    def b_copy(j):
        return pltpu.make_async_remote_copy(
            src_ref=bsend.at[j], dst_ref=brecv.at[j], send_sem=b_ssem.at[j], recv_sem=b_rsem.at[j],
            device_id=(x, (z * 2 + 1 - y) * 2 + core), device_id_type=MESH)

    def c_copy(j):
        return pltpu.make_async_remote_copy(
            src_ref=csend.at[j], dst_ref=crecv.at[j], send_sem=c_ssem.at[j], recv_sem=c_rsem.at[j],
            device_id=(x, (lax.rem(z + 1 + j, nz) * 2 + y) * 2 + core), device_id_type=MESH)

    def step(t, _):
        @pl.when(t < chunks)
        def _():
            w_copy(t).wait()
            prod = jnp.dot(hid[...], wbuf[t], preferred_element_type=jnp.float32)
            ykeep[t, 0] = prod[:group_rows]
            ykeep[t, 1] = prod[group_rows:]
            asend[t] = ykeep[t, 1 - keep].astype(jnp.bfloat16)
            a_copy(t).start()

        u = t - LAG_A

        @pl.when(jnp.logical_and(u >= 0, u < chunks))
        def _():
            a_copy(u).wait_recv()
            total = ykeep[u, keep] + arecv[u].astype(jnp.float32)
            j = u // 2

            @pl.when(u % 2 == 0)
            def _():
                bsend[j] = total.astype(jnp.bfloat16)
                b_copy(j).start()

            @pl.when(u % 2 == 1)
            def _():
                bkeep[j] = total

        v = t - LAG_A - LAG_B

        @pl.when(jnp.logical_and(v >= 0, v % 2 == 1))
        def _():
            j = v // 2
            b_copy(j).wait_recv()
            both = bkeep[j] + brecv[j].astype(jnp.float32)

            @pl.when(j < nz - 1)
            def _():
                csend[j] = both.astype(jnp.bfloat16)
                c_copy(j).start()

            @pl.when(j == nz - 1)
            def _():
                own[...] = both

        return 0

    lax.fori_loop(0, chunks + LAG_A + LAG_B, step, 0)

    for j in range(nz - 1):
        c_copy(j).wait_recv()
    total = own[...]
    for j in range(nz - 1):
        total = total + crecv[j].astype(jnp.float32)
    for q in range(n):
        fin[q] = total[q * rows:(q + 1) * rows].astype(jnp.bfloat16)

    def f_copy(q, x_part, chunk):
        return pltpu.make_async_remote_copy(
            src_ref=fin.at[q], dst_ref=out_ref.at[:, cols_of(x_part, chunk)], send_sem=f_ssem.at[q],
            recv_sem=f_rsem.at[x_part * chunks + chunk], device_id=(core, q), device_id_type=MESH)

    mine = pltpu.make_async_copy(fin.at[p], out_ref.at[:, cols_of(x, chip)], fl_sem)

    @pl.when(x == core)
    def _():
        mine.start()

    def each_final(q, act):
        @pl.when(jnp.logical_or(x != core, q != p))
        def _():
            act(f_copy(q, x, chip))

    def start_final(i, _):
        each_final(lax.rem(p + i, n), lambda c: c.start())
        return 0

    lax.fori_loop(0, n, start_final, 0)

    def wait_final(i, _):
        x_part, chunk = i // chunks, lax.rem(i, chunks)

        @pl.when(jnp.logical_or(x_part != x, chunk * 2 + x != p))
        def _():
            f_copy(i, x_part, chunk).wait_recv()

        return 0

    lax.fori_loop(0, n, wait_final, 0)

    @pl.when(x == core)
    def _():
        mine.wait()

    def end_up(d, _):
        up_copy(d, p).wait_send()
        return 0

    def end_a(t, _):
        a_copy(t).wait_send()
        return 0

    def end_final(q, _):
        each_final(q, lambda c: c.wait_send())
        return 0

    lax.fori_loop(1, n, end_up, 0)
    for s in range(n):
        forward(s).wait_send()
    lax.fori_loop(0, chunks, end_a, 0)
    for j in range(nz):
        b_copy(j).wait_send()
    for j in range(nz - 1):
        c_copy(j).wait_send()
    lax.fori_loop(0, n, end_final, 0)


def fused_body(n, up_pre, down_weight):
    rows = up_pre.shape[0]
    depth, model = down_weight.shape
    nz, chunks, tokens = n // 4, n // 2, rows * n
    width = model // n
    bf, f32, dma = jnp.bfloat16, jnp.float32, pltpu.SemaphoreType.DMA
    return pl.pallas_call(
        functools.partial(kernel, n),
        out_shape=jax.ShapeDtypeStruct((rows, model), bf),
        in_specs=[pl.BlockSpec(memory_space=pl.ANY)] * 2,
        out_specs=pl.BlockSpec(memory_space=pl.ANY),
        scratch_shapes=[
            pltpu.VMEM((chunks, depth, width), bf),
            pltpu.VMEM((2, n, rows, depth), bf),
            pltpu.VMEM((2 * tokens, depth), f32),
            pltpu.VMEM((2 * tokens, depth), bf),
            pltpu.VMEM((chunks, 2, tokens, width), f32),
            pltpu.VMEM((chunks, tokens, width), bf),
            pltpu.VMEM((chunks, tokens, width), bf),
            pltpu.VMEM((nz, tokens, width), f32),
            pltpu.VMEM((nz, tokens, width), bf),
            pltpu.VMEM((nz, tokens, width), bf),
            pltpu.VMEM((nz - 1, tokens, width), bf),
            pltpu.VMEM((nz - 1, tokens, width), bf),
            pltpu.VMEM((tokens, width), f32),
            pltpu.VMEM((n, rows, width), bf),
            dma((chunks,)), dma((n,)), dma((n,)), dma((n,)), dma((n,)), dma,
            dma((chunks,)), dma((chunks,)), dma((nz,)), dma((nz,)), dma((nz - 1,)), dma((nz - 1,)),
            dma((n,)), dma((n,)), dma,
        ],
        compiler_params=pltpu.CompilerParams(collective_id=0, has_side_effects=True, vmem_limit_bytes=60 * 2 ** 20),
        cost_estimate=pl.CostEstimate(flops=4 * tokens * depth * model // 2, bytes_accessed=depth * model, transcendentals=0),
    )(up_pre, down_weight)


def solution(mesh):
    in_specs = (P(("groups", "mp"), None), P("mp", None))
    out_specs = P(("groups", "mp"), None)
    n = mesh.shape["mp"]

    def body(up_pre, down_weight):
        depth, model = down_weight.shape
        resident = depth * model
        fits = mesh.shape["groups"] == 2 and n == 16 and (up_pre.shape[0] * n) % 16 == 0
        if fits and model % (128 * n) == 0 and depth % 128 == 0 and resident <= 44 * 2 ** 20:
            return fused_body(n, up_pre, down_weight)
        return plain_body(up_pre, down_weight)

    return jax.shard_map(body, mesh=mesh, in_specs=in_specs, out_specs=out_specs, check_vma=False)
```
